32 devices in a mesh: grp: 4 (over x, core), dp: 8 (over z, y).
Axes of the slice: x: 2, y: 2, z: 4, core: 2. Of those that a mesh axis runs over, the one named last changes fastest.
Arguments:
- normed: bfloat16 [16384, 1280], P(('grp', 'dp')), may hold values from -6 to 6
- w_in: bfloat16 [5120, 1280], replicated, may hold values from -0.15625 to 0.15625
- w_out: bfloat16 [1280, 2560], replicated, may hold values from -0.125 to 0.125
- cotangent: bfloat16 [16384, 1280], P(('grp', 'dp')), may hold values from -6 to 6
Outputs:
- grad_in: float32 [5120, 1280], P('dp')
- grad_out: float32 [1280, 2560], P('dp')
- grad_normed: bfloat16 [16384, 1280], P(('grp', 'dp'))
The draws below stay inside these ranges and needn't reach their ends.
All inputs are finite; a program needn't handle non-finite values.
Results may differ from the reference program's by a relative error of at most 0.005.
Values sent between devices are 32-bit elements; how exact they have to be, the bound alone decides.
A program may use at most 192 MiB of HBM per device.

```python
import jax
import jax.numpy as jnp
from jax import lax

D = 1280
FW = 2560
TOK_DEV = 512
TOKENS = 16384


def strengthened(values, key, source, target, shards_of, factor):
    owner, partner = [(jnp.arange(values.shape[axis_at]) // (values.shape[axis_at] // shards_of)).reshape([-1 if axis == axis_at else 1 for axis in range(values.ndim)]) for axis_at in (source, target)]
    chosen = jax.random.permutation(key, shards_of)[partner]
    strong = (owner == chosen) | (owner == (partner + shards_of // 2) % shards_of)
    return jnp.where(strong, factor * values, values)


def shard_levels(key, extent, pieces, least, high):
    def one(axis_at, shards_of):
        draws = jax.random.uniform(jax.random.fold_in(jax.random.fold_in(key, 6), axis_at), (shards_of,), jnp.float32, least / len(pieces), high / len(pieces))
        return jnp.repeat(jnp.exp(draws), extent[axis_at] // shards_of).reshape((-1,) + (1,) * (len(extent) - axis_at - 1))

    factor_of = one(*pieces[0])
    for cut in pieces[1:]:
        factor_of = factor_of * one(*cut)
    return factor_of


def scatter_about(rng, extent, deviation, limit, split=(), dtype=jnp.bfloat16):
    values = jax.random.normal(rng, extent, jnp.float32) * deviation
    if len(split) > 0:
        values = shard_levels(rng, extent, split, -0.22, 0.18) * values
    return jnp.clip(values, min=-limit, max=limit).astype(dtype)


def bell_draw_with(rng, dims, deviation, reach, cuts, heavy, kind=jnp.bfloat16):
    array = deviation * jax.random.normal(rng, dims, jnp.float32)
    if cuts:
        array = array * shard_levels(rng, dims, cuts, -0.22, 0.18)
    return jnp.clip(strengthened(array, jax.random.fold_in(rng, 3), *heavy), -reach, reach).astype(kind)


def setup_inputs(seed: int = 0) -> dict:
    arg_keys = jax.random.split(jax.random.key(seed), 5)
    normed = scatter_about(arg_keys[0], (TOKENS, D), 1.0, 6.0, ((0, 32),))
    w_in = scatter_about(arg_keys[1], (2 * FW, D), D ** -0.5, 0.15625)
    w_out = scatter_about(arg_keys[2], (D, FW), FW ** -0.5, 0.125)
    cotangent = bell_draw_with(arg_keys[3], (TOKENS, D), 1.0, 6.0, ((0, 32),), (0, 1, 32, 2.75))
    return {"normed": normed, "w_in": w_in, "w_out": w_out, "cotangent": cotangent}


def cross_dot(left, right):
    return lax.dot_general(left, right, (((0,), (0,)), ((), ())), preferred_element_type=jnp.float32)


def block_terms(normed, w_in, w_out, cotangent):
    width = w_out.shape[1]
    proj = lax.dot_general(normed, w_in, (((1,), (1,)), ((), ())), preferred_element_type=jnp.float32)
    value = proj[:, :width]
    gate = proj[:, width:]
    cdf = 0.5 * (1.0 + lax.erf(gate * (2.0 ** -0.5)))
    density = jnp.exp(-0.5 * gate * gate) * ((2.0 * jnp.pi) ** -0.5)
    act = (value * gate * cdf).astype(jnp.bfloat16)
    dact = jnp.dot(cotangent, w_out, preferred_element_type=jnp.float32)
    d_value = dact * gate * cdf
    d_gate = dact * value * (cdf + gate * density)
    dproj = jnp.concatenate([d_value, d_gate], axis=1).astype(jnp.bfloat16)
    grad_normed = jnp.dot(dproj, w_in, preferred_element_type=jnp.float32).astype(jnp.bfloat16)
    return cross_dot(dproj, normed), cross_dot(cotangent, act), grad_normed


def reference(normed, w_in, w_out, cotangent):
    blocks = TOKENS // TOK_DEV
    normed_blocks = normed.reshape(blocks, TOK_DEV, D)
    cot_blocks = cotangent.reshape(blocks, TOK_DEV, D)

    def step(carry, pair):
        sum_in, sum_out = carry
        term_in, term_out, grad_block = block_terms(pair[0], w_in, w_out, pair[1])
        return (sum_in + term_in, sum_out + term_out), grad_block

    start = (jnp.zeros((2 * FW, D), jnp.float32), jnp.zeros((D, FW), jnp.float32))
    (sum_in, sum_out), grads = lax.scan(step, start, (normed_blocks, cot_blocks))
    factor = TOKENS ** -0.5
    return sum_in * factor, sum_out * factor, grads.reshape(TOKENS, D)
```

```python
import functools

import jax
import jax.numpy as jnp
from jax import lax
from jax.experimental import pallas as pl
from jax.experimental.pallas import tpu as pltpu
from jax.sharding import PartitionSpec as P

MESH = pl.DeviceIdType.MESH


def greet(partners):
    barrier = pltpu.get_barrier_semaphore()
    for partner in partners:
        pl.semaphore_signal(barrier, inc=1, device_id=partner, device_id_type=MESH)
    pl.semaphore_wait(barrier, len(partners))


def trade_kernel(normed, cot, all_normed, all_cot, mine, theirs, send_sem, recv_sem):
    grp = lax.axis_index("grp")
    dp = lax.axis_index("dp")
    other = (grp + 1 - 2 * lax.rem(grp, 2), dp)
    rows = normed.shape[0]
    mine[0] = normed[...].astype(jnp.float32)
    mine[1] = cot[...].astype(jnp.float32)
    greet([other])
    copies = [
        pltpu.make_async_remote_copy(
            src_ref=mine.at[k], dst_ref=theirs.at[k], send_sem=send_sem.at[k],
            recv_sem=recv_sem.at[k], device_id=other, device_id_type=MESH,
        )
        for k in range(2)
    ]
    for copy in copies:
        copy.start()
    all_normed[:rows] = normed[...]
    all_cot[:rows] = cot[...]
    copies[0].wait_recv()
    all_normed[rows:] = theirs[0].astype(jnp.bfloat16)
    copies[1].wait_recv()
    all_cot[rows:] = theirs[1].astype(jnp.bfloat16)
    for copy in copies:
        copy.wait_send()


def trade(normed, cot):
    rows, width = normed.shape
    whole = jax.ShapeDtypeStruct((2 * rows, width), jnp.bfloat16)
    vmem = pl.BlockSpec(memory_space=pltpu.VMEM)
    return pl.pallas_call(
        trade_kernel,
        out_shape=(whole, whole),
        in_specs=[vmem, vmem],
        out_specs=(vmem, vmem),
        scratch_shapes=[
            pltpu.VMEM((2, rows, width), jnp.float32),
            pltpu.VMEM((2, rows, width), jnp.float32),
            pltpu.SemaphoreType.DMA((2,)),
            pltpu.SemaphoreType.DMA((2,)),
        ],
        compiler_params=pltpu.CompilerParams(
            collective_id=0, has_side_effects=True, vmem_limit_bytes=40 * 2**20
        ),
        name="trade_tokens",
    )(normed, cot)


def sum_kernel(
    n, factor, dprojt, normed, cott, actt, out_r, out_x,
    part_r, part_x, land_r, land_e, land_x, final_r, land_p,
    ring_r, ring_x, halves, pair_r, core_r, spread,
):
    grp = lax.axis_index("grp")
    dp = lax.axis_index("dp")
    x, core = grp // 2, lax.rem(grp, 2)
    half = n // 2
    up = lax.rem(dp, 2)
    pos = jnp.where(up == 0, dp // 2, n - 1 - dp // 2)

    def member(place):
        place = lax.rem(place + 2 * n, n)
        return jnp.where(place < half, 2 * place, 2 * (n - 1 - place) + 1)

    following, previous = (grp, member(pos + 1)), (grp, member(pos - 1))
    along_x = ((1 - x) * 2 + core, dp)
    other = (x * 2 + 1 - core, dp)
    greet([following, previous, along_x, other])
    onward = (following, previous)

    go = cott.shape[1]
    rows_r = part_r.shape[2]
    rows_h = part_x.shape[3]
    cols = part_r.shape[3]
    split = rows_r - go

    def dot(left, right, axis):
        return lax.dot_general(
            left, right, (((1,), (axis,)), ((), ())), preferred_element_type=jnp.float32
        )

    def owner(way, s):
        return member(pos - 1 - s) if way == 0 else member(pos + 1 + s)

    def compute_r(s):
        for way in range(2):
            d = owner(way, s)
            span = slice(way * cols, (way + 1) * cols)
            part_r[way, s, :go] = dot(cott[d], actt[span, :], 1)
            part_r[way, s, go:] = dot(dprojt[d, :split], normed[:, span], 0)

    def compute_x(s):
        for way in range(2):
            d = owner(way, s)
            span = slice(way * cols, (way + 1) * cols)
            term = dot(dprojt[d, split:], normed[:, span], 0)
            part_x[0, s, way] = term[:rows_h]
            part_x[1, s, way] = term[rows_h:]

    def remote(src, dst, sems, where, device):
        return pltpu.make_async_remote_copy(
            src_ref=src, dst_ref=dst, send_sem=sems.at[(0,) + where],
            recv_sem=sems.at[(1,) + where], device_id=device, device_id_type=MESH,
        )

    def hop_r(way, s, first=False):
        src = part_r.at[way, 0] if first else land_r.at[way, s - 1]
        return remote(src, land_r.at[way, s], ring_r, (way, s), onward[way])

    def hop_x(way, s, first=False):
        src = land_e.at[0, way] if first else land_x.at[way, s - 1]
        return remote(src, land_x.at[way, s], ring_x, (way, s), onward[way])

    def give_half(s):
        return remote(part_x.at[1 - x, s], land_e.at[s], halves, (s,), along_x)

    def loop(first, last, body):
        def step(s, carry):
            body(s)
            return carry

        lax.fori_loop(first, last, step, 0)

    compute_r(0)
    for way in range(2):
        hop_r(way, 0, True).start()

    def make_x(s):
        compute_x(s)
        give_half(s).start()

    loop(0, n, make_x)
    loop(1, n, compute_r)

    def step_r(s):
        for way in range(2):
            hop_r(way, s, True).wait_recv()
            land_r[way, s] = land_r[way, s] + part_r[way, s + 1]
            hop_r(way, s + 1).start()

    def step_x(s):
        give_half(s + 1).wait_recv()
        for way in range(2):
            hop_x(way, s, True).wait_recv()
            land_x[way, s] = land_x[way, s] + (part_x[x, s + 1, way] + land_e[s + 1, way])
            hop_x(way, s + 1).start()

    def step_both(s):
        step_r(s)
        step_x(s - lag)

    lag = min(n // 2, n - 2)
    loop(0, lag, step_r)
    give_half(0).wait_recv()
    for way in range(2):
        land_e[0, way] = land_e[0, way] + part_x[x, 0, way]
        hop_x(way, 0, True).start()
    loop(lag, n - 2, step_both)

    def swap_r(way):
        return remote(final_r.at[way], land_p.at[way], pair_r, (way,), along_x)

    def tell_r(way):
        return remote(out_r.at[core, way], out_r.at[core, way], core_r, (way,), other)

    def hear_r(way):
        return remote(out_r.at[1 - core, way], out_r.at[1 - core, way], core_r, (way,), other)

    for way in range(2):
        hop_r(way, n - 2, True).wait_recv()
        final_r[way] = (land_r[way, n - 2] + part_r[way, n - 1]) * factor
        swap_r(way).start()

    loop(n - 2 - lag, n - 2, step_x)

    def show(which, c, h, way, device):
        spot = out_x.at[c, h, way]
        return remote(spot, spot, spread, (which, way), device)

    give_half(n - 1).wait_recv()
    for way in range(2):
        hop_x(way, n - 2, True).wait_recv()
        out_x[core, x, way] = (
            land_x[way, n - 2] + (part_x[x, n - 1, way] + land_e[n - 1, way])
        ) * factor
        show(0, core, x, way, along_x).start()
        show(1, core, x, way, other).start()
    for way in range(2):
        swap_r(way).wait_recv()
        out_r[core, way] = final_r[way] + land_p[way]
        tell_r(way).start()
    for way in range(2):
        show(0, core, 1 - x, way, along_x).wait_recv()
        show(2, core, 1 - x, way, other).start()
    for way in range(2):
        hear_r(way).wait_recv()
        show(1, 1 - core, x, way, other).wait_recv()
        show(2, 1 - core, 1 - x, way, other).wait_recv()

    def drain(s):
        for way in range(2):
            hop_r(way, s, True).wait_send()
            hop_x(way, s, True).wait_send()

    loop(0, n - 1, drain)
    loop(0, n, lambda s: give_half(s).wait_send())
    for way in range(2):
        swap_r(way).wait_send()
        tell_r(way).wait_send()
        show(0, core, x, way, along_x).wait_send()
        show(1, core, x, way, other).wait_send()
        show(2, core, 1 - x, way, other).wait_send()


def sum_all(n, factor, dprojt, normed, cott, actt):
    gi, go, width = dprojt.shape[1], cott.shape[1], normed.shape[1]
    rows = gi + go
    rows_x = rows * 7 // 15 // 32 * 32
    rows_r, rows_h, cols = rows - rows_x, rows_x // 2, width // 2
    vmem = pl.BlockSpec(memory_space=pltpu.VMEM)
    f32 = jnp.float32
    dma = pltpu.SemaphoreType.DMA
    tokens = normed.shape[0]
    return pl.pallas_call(
        functools.partial(sum_kernel, n, factor),
        out_shape=(
            jax.ShapeDtypeStruct((2, 2, rows_r, cols), f32),
            jax.ShapeDtypeStruct((2, 2, 2, rows_h, cols), f32),
        ),
        in_specs=[vmem] * 4,
        out_specs=(vmem, vmem),
        scratch_shapes=[
            pltpu.VMEM((2, n, rows_r, cols), f32),
            pltpu.VMEM((2, n, 2, rows_h, cols), f32),
            pltpu.VMEM((2, n - 1, rows_r, cols), f32),
            pltpu.VMEM((n, 2, rows_h, cols), f32),
            pltpu.VMEM((2, n - 1, rows_h, cols), f32),
            pltpu.VMEM((2, rows_r, cols), f32),
            pltpu.VMEM((2, rows_r, cols), f32),
            dma((2, 2, n - 1)),
            dma((2, 2, n - 1)),
            dma((2, n)),
            dma((2, 2)),
            dma((2, 2)),
            dma((2, 3, 2)),
        ],
        compiler_params=pltpu.CompilerParams(
            collective_id=1, has_side_effects=True, vmem_limit_bytes=62 * 2**20
        ),
        cost_estimate=pl.CostEstimate(
            flops=2 * n * rows * tokens * width, bytes_accessed=20 * 2**20, transcendentals=0
        ),
        name="sum_gradients",
    )(dprojt, normed, cott, actt)


def local(normed, w_in, w_out, cotangent):
    width = w_out.shape[1]
    model = w_in.shape[1]
    n = lax.axis_size("dp")
    outer = lax.axis_size("grp")
    tokens = normed.shape[0]
    factor = (tokens * n * outer) ** (-0.5)
    core = lax.rem(lax.axis_index("grp"), 2)
    gi = 2 * width // n // 2
    go = model // n
    units = width // 2

    w_in_c = lax.dynamic_index_in_dim(
        w_in.reshape(n, 2, gi, model), core, 1, keepdims=False
    ).reshape(2 * units, model)
    w_out_c = lax.dynamic_index_in_dim(
        w_out.reshape(model, n // 2, 2, gi), core, 2, keepdims=False
    ).reshape(model, units)

    both, both_cot = trade(normed, cotangent)
    projt = lax.dot_general(
        w_in_c, both, (((1,), (1,)), ((), ())), preferred_element_type=jnp.float32
    )
    value, gate = projt[:units], projt[units:]
    cdf = 0.5 * (1.0 + lax.erf(gate * 2.0 ** (-0.5)))
    density = jnp.exp(-0.5 * gate * gate) * (2.0 * jnp.pi) ** (-0.5)
    actt = (value * gate * cdf).astype(jnp.bfloat16)
    dactt = lax.dot_general(
        w_out_c, both_cot, (((0,), (1,)), ((), ())), preferred_element_type=jnp.float32
    )
    d_value = dactt * gate * cdf
    d_gate = dactt * value * (cdf + gate * density)
    dprojt = jnp.concatenate([d_value, d_gate], axis=0).astype(jnp.bfloat16)

    share = lax.dot_general(
        dprojt, w_in_c, (((0,), (0,)), ((), ())), preferred_element_type=jnp.float32
    )
    pairs = [(i, i + 1 - 2 * (i % 2)) for i in range(outer)]
    came = lax.ppermute(share[tokens:], "grp", pairs)
    grad_normed = (share[:tokens] + came).astype(jnp.bfloat16)

    sum_r, sum_x = sum_all(
        n, factor, dprojt.reshape(n, gi, 2 * tokens), both,
        both_cot.T.reshape(n, go, 2 * tokens), actt,
    )
    rows_r = sum_r.shape[2]
    wide_r = sum_r.transpose(0, 2, 1, 3).reshape(2, rows_r, model)
    wide_x = sum_x.transpose(0, 1, 3, 2, 4).reshape(2, -1, model)
    grad_in = jnp.concatenate([wide_r[:, go:], wide_x], axis=1).reshape(2 * gi, model)
    grad_out = (
        wide_r[:, :go].reshape(2, go, n // 2, gi).transpose(1, 2, 0, 3).reshape(go, width)
    )
    return (grad_in, grad_out, grad_normed)


def solution(mesh):
    placed = (P(("grp", "dp"), None), P(), P(), P(("grp", "dp"), None))
    return jax.shard_map(
        local,
        mesh=mesh,
        in_specs=placed,
        out_specs=(P("dp", None), P("dp", None), P(("grp", "dp"), None)),
        check_vma=False,
    )
```

```python
import functools

import jax
import jax.numpy as jnp
from jax import lax
from jax.experimental import pallas as pl
from jax.experimental.pallas import tpu as pltpu
from jax.sharding import PartitionSpec as P

MESH = pl.DeviceIdType.MESH


def greet(partners):
    barrier = pltpu.get_barrier_semaphore()
    for partner in partners:
        pl.semaphore_signal(barrier, inc=1, device_id=partner, device_id_type=MESH)
    pl.semaphore_wait(barrier, len(partners))


def trade_kernel(normed, cot, all_normed, all_cot, mine, theirs, send_sem, recv_sem):
    grp = lax.axis_index("grp")
    dp = lax.axis_index("dp")
    other = (grp + 1 - 2 * lax.rem(grp, 2), dp)
    rows = normed.shape[0]
    mine[0] = normed[...].astype(jnp.float32)
    mine[1] = cot[...].astype(jnp.float32)
    greet([other])
    copies = [
        pltpu.make_async_remote_copy(
            src_ref=mine.at[k], dst_ref=theirs.at[k], send_sem=send_sem.at[k],
            recv_sem=recv_sem.at[k], device_id=other, device_id_type=MESH,
        )
        for k in range(2)
    ]
    for copy in copies:
        copy.start()
    all_normed[:rows] = normed[...]
    all_cot[:rows] = cot[...]
    copies[0].wait_recv()
    all_normed[rows:] = theirs[0].astype(jnp.bfloat16)
    copies[1].wait_recv()
    all_cot[rows:] = theirs[1].astype(jnp.bfloat16)
    for copy in copies:
        copy.wait_send()


def trade(normed, cot):
    rows, width = normed.shape
    whole = jax.ShapeDtypeStruct((2 * rows, width), jnp.bfloat16)
    vmem = pl.BlockSpec(memory_space=pltpu.VMEM)
    return pl.pallas_call(
        trade_kernel,
        out_shape=(whole, whole),
        in_specs=[vmem, vmem],
        out_specs=(vmem, vmem),
        scratch_shapes=[
            pltpu.VMEM((2, rows, width), jnp.float32),
            pltpu.VMEM((2, rows, width), jnp.float32),
            pltpu.SemaphoreType.DMA((2,)),
            pltpu.SemaphoreType.DMA((2,)),
        ],
        compiler_params=pltpu.CompilerParams(
            collective_id=0, has_side_effects=True, vmem_limit_bytes=40 * 2**20
        ),
        name="trade_tokens",
    )(normed, cot)


def sum_kernel(
    n, factor, dprojt, normed, cott, actt, w_in, out_in, out_out, out_normed,
    part_r, part_e, land_r, land_e, land_x, final_r, land_p, land_o, share, land_s, w_now,
    ring_r, ring_x, halves, pair_r, core_r, core_o, spread, core_s, fetch,
):
    grp = lax.axis_index("grp")
    dp = lax.axis_index("dp")
    x, core = grp // 2, lax.rem(grp, 2)
    half = n // 2
    up = lax.rem(dp, 2)
    pos = jnp.where(up == 0, dp // 2, n - 1 - dp // 2)

    def member(place):
        place = lax.rem(place + 2 * n, n)
        return jnp.where(place < half, 2 * place, 2 * (n - 1 - place) + 1)

    following, previous = (grp, member(pos + 1)), (grp, member(pos - 1))
    along_x = ((1 - x) * 2 + core, dp)
    other = (x * 2 + 1 - core, dp)
    greet([following, previous, along_x, other])
    onward = (following, previous)

    gi, go = dprojt.shape[1], cott.shape[1]
    rows_r = part_r.shape[1]
    rows_h, cols = land_e.shape[2:]
    split = rows_r - go
    spans = (slice(0, cols), slice(cols, 2 * cols))

    def dot(left, right, axes):
        return lax.dot_general(
            left, right, (((axes[0],), (axes[1],)), ((), ())),
            preferred_element_type=jnp.float32,
        )

    def owner(way, s):
        return member(pos - 1 - s) if way == 0 else member(pos + 1 + s)

    def compute_r(way, s):
        d = owner(way, s)
        part_r[way, :go] = dot(cott[d], actt[spans[way], :], (1, 1))
        part_r[way, go:] = dot(dprojt[d, :split], normed[:, spans[way]], (1, 0))

    def rows_of_half(h):
        return pl.ds(pl.multiple_of(split + h * rows_h, 16), rows_h)

    def compute_x(way, s, h):
        d = owner(way, s)
        return dot(dprojt[d, rows_of_half(h)], normed[:, spans[way]], (1, 0))

    def remote(src, dst, sems, where, device):
        return pltpu.make_async_remote_copy(
            src_ref=src, dst_ref=dst, send_sem=sems.at[(0,) + where],
            recv_sem=sems.at[(1,) + where], device_id=device, device_id_type=MESH,
        )

    def hop_r(way, s, first=False):
        src = final_r.at[way] if first else land_r.at[way, s - 1]
        return remote(src, land_r.at[way, s], ring_r, (way, s), onward[way])

    def hop_x(way, s, first=False):
        src = land_e.at[0, way] if first else land_x.at[way, s - 1]
        return remote(src, land_x.at[way, s], ring_x, (way, s), onward[way])

    def give_half(s):
        return remote(part_e.at[s], land_e.at[s], halves, (s,), along_x)

    def loop(first, last, body):
        def step(s, carry):
            body(s)
            return carry

        lax.fori_loop(first, last, step, 0)

    for way in range(2):
        compute_r(way, 0)
        final_r[way] = part_r[way]
        hop_r(way, 0, True).start()

    def make_x(s):
        for way in range(2):
            part_e[s, way] = compute_x(way, s, 1 - x)
        give_half(s).start()

    loop(0, n, make_x)

    tokens = out_normed.shape[0]

    def add_share(d, k, total):
        copy = pltpu.make_async_copy(w_in.at[d], w_now, fetch)
        copy.start()
        copy.wait()
        rows = slice(k * tokens, (k + 1) * tokens)
        for span in spans:
            total[:, span] += dot(dprojt[d, :, rows], w_now[:, span], (0, 0))

    share[...] = jnp.zeros_like(share)
    loop(0, n, lambda d: add_share(d, 1, share))
    give_share = remote(share, land_s, core_s, (), other)
    give_share.start()

    def step_r(s):
        for way in range(2):
            compute_r(way, s + 1)
        for way in range(2):
            hop_r(way, s, True).wait_recv()
            land_r[way, s] = land_r[way, s] + part_r[way]
            hop_r(way, s + 1).start()

    def step_first(s):
        step_r(s)
        add_share(s, 0, land_s)

    def own_x(way, s):
        return compute_x(way, s, x) + land_e[s, way]

    def step_x(s):
        give_half(s + 1).wait_recv()
        for way in range(2):
            land_e[s + 1, way] = own_x(way, s + 1)
        for way in range(2):
            hop_x(way, s, True).wait_recv()
            land_x[way, s] = land_x[way, s] + land_e[s + 1, way]
            hop_x(way, s + 1).start()

    def step_both(s):
        step_r(s)
        step_x(s - lag)
        add_share(s, 0, land_s)

    lag = min(n // 2, n - 2)
    step_r(0)
    give_share.wait_recv()
    for d in (0, n - 2, n - 1):
        add_share(d, 0, land_s)
    loop(1, lag, step_first)
    give_half(0).wait_recv()
    for way in range(2):
        land_e[0, way] = own_x(way, 0)
        hop_x(way, 0, True).start()
    loop(lag, n - 2, step_both)

    out_normed[...] = land_s[...].astype(out_normed.dtype)

    def swap_r(way):
        return remote(part_r.at[way], land_p.at[way], pair_r, (way,), along_x)

    for way in range(2):
        compute_r(way, n - 1)
        hop_r(way, n - 2, True).wait_recv()
        part_r[way] = (land_r[way, n - 2] + part_r[way]) * factor
        swap_r(way).start()

    loop(n - 2 - lag, n - 2, step_x)

    def tell_r(c, way):
        spot = out_in.at[c, :split, spans[way]]
        return remote(spot, spot, core_r, (way,), other)

    def tell_o(way):
        return remote(final_r.at[way, :go], land_o.at[way], core_o, (way,), other)

    def show(which, c, h, way, device):
        rows = pl.ds(pl.multiple_of(split + h * rows_h, 8), rows_h)
        spot = out_in.at[c, rows, spans[way]]
        return remote(spot, spot, spread, (which, way), device)

    give_half(n - 1).wait_recv()
    for way in range(2):
        land_e[n - 1, way] = own_x(way, n - 1)
    rows_x = pl.ds(pl.multiple_of(split + x * rows_h, 8), rows_h)
    for way in range(2):
        hop_x(way, n - 2, True).wait_recv()
        out_in[core, rows_x, spans[way]] = (
            land_x[way, n - 2] + land_e[n - 1, way]
        ) * factor
        show(0, core, x, way, along_x).start()
        show(1, core, x, way, other).start()
    for way in range(2):
        swap_r(way).wait_recv()
        hop_r(way, 0, True).wait_send()
        final_r[way, :go] = part_r[way, :go] + land_p[way, :go]
        tell_o(way).start()
        out_in[core, :split, spans[way]] = part_r[way, go:] + land_p[way, go:]
        tell_r(core, way).start()
    for way in range(2):
        show(0, core, 1 - x, way, along_x).wait_recv()
        show(2, core, 1 - x, way, other).start()
    for way in range(2):
        tell_o(way).wait_recv()
    mine = jnp.concatenate([final_r[0, :go], final_r[1, :go]], axis=1)
    theirs = jnp.concatenate([land_o[0], land_o[1]], axis=1)
    first = jnp.where(core == 0, mine, theirs)
    second = jnp.where(core == 0, theirs, mine)
    out_out[...] = jnp.concatenate(
        [
            block[:, b * gi : (b + 1) * gi]
            for b in range(half)
            for block in (first, second)
        ],
        axis=1,
    )
    for way in range(2):
        tell_r(1 - core, way).wait_recv()
        show(1, 1 - core, x, way, other).wait_recv()
        show(2, 1 - core, 1 - x, way, other).wait_recv()

    def drain(s):
        for way in range(2):
            hop_r(way, s + 1).wait_send()
            hop_x(way, s, True).wait_send()

    loop(0, n - 2, drain)
    for way in range(2):
        hop_x(way, n - 2, True).wait_send()
    loop(0, n, lambda s: give_half(s).wait_send())
    give_share.wait_send()
    for way in range(2):
        swap_r(way).wait_send()
        tell_o(way).wait_send()
        tell_r(core, way).wait_send()
        show(0, core, x, way, along_x).wait_send()
        show(1, core, x, way, other).wait_send()
        show(2, core, 1 - x, way, other).wait_send()


def sum_all(n, factor, dprojt, normed, cott, actt, w_in):
    gi, go, width = dprojt.shape[1], cott.shape[1], normed.shape[1]
    units = actt.shape[0]
    rows = gi + go
    rows_x = rows * 7 // 15 // 32 * 32
    rows_r, rows_h, cols = rows - rows_x, rows_x // 2, width // 2
    vmem = pl.BlockSpec(memory_space=pltpu.VMEM)
    f32 = jnp.float32
    dma = pltpu.SemaphoreType.DMA
    tokens = normed.shape[0] // 2
    return pl.pallas_call(
        functools.partial(sum_kernel, n, factor),
        out_shape=(
            jax.ShapeDtypeStruct((2, gi, width), f32),
            jax.ShapeDtypeStruct((go, 2 * units), f32),
            jax.ShapeDtypeStruct((tokens, width), jnp.bfloat16),
        ),
        in_specs=[vmem] * 4 + [pl.BlockSpec(memory_space=pl.ANY)],
        out_specs=(vmem,) * 3,
        scratch_shapes=[
            pltpu.VMEM((2, rows_r, cols), f32),
            pltpu.VMEM((n, 2, rows_h, cols), f32),
            pltpu.VMEM((2, n - 1, rows_r, cols), f32),
            pltpu.VMEM((n, 2, rows_h, cols), f32),
            pltpu.VMEM((2, n - 1, rows_h, cols), f32),
            pltpu.VMEM((2, rows_r, cols), f32),
            pltpu.VMEM((2, rows_r, cols), f32),
            pltpu.VMEM((2, go, cols), f32),
            pltpu.VMEM((tokens, width), f32),
            pltpu.VMEM((tokens, width), f32),
            pltpu.VMEM((gi, width), jnp.bfloat16),
            dma((2, 2, n - 1)),
            dma((2, 2, n - 1)),
            dma((2, n)),
            dma((2, 2)),
            dma((2, 2)),
            dma((2, 2)),
            dma((2, 3, 2)),
            dma((2,)),
            dma,
        ],
        compiler_params=pltpu.CompilerParams(
            collective_id=1, has_side_effects=True, vmem_limit_bytes=62 * 2**20
        ),
        cost_estimate=pl.CostEstimate(
            flops=6 * n * rows * tokens * width, bytes_accessed=20 * 2**20, transcendentals=0
        ),
        name="sum_gradients",
    )(dprojt, normed, cott, actt, w_in)


def local(normed, w_in, w_out, cotangent):
    width = w_out.shape[1]
    model = w_in.shape[1]
    n = lax.axis_size("dp")
    outer = lax.axis_size("grp")
    tokens = normed.shape[0]
    factor = (tokens * n * outer) ** (-0.5)
    core = lax.rem(lax.axis_index("grp"), 2)
    gi = 2 * width // n // 2
    go = model // n
    units = width // 2

    w_in_c = lax.dynamic_index_in_dim(
        w_in.reshape(n, 2, gi, model), core, 1, keepdims=False
    )
    w_out_c = lax.dynamic_index_in_dim(
        w_out.T.reshape(n // 2, 2, gi, model), core, 1, keepdims=False
    ).reshape(units, model)

    both, both_cot = trade(normed, cotangent)
    projt = lax.dot_general(
        w_in_c.reshape(2 * units, model), both, (((1,), (1,)), ((), ())),
        preferred_element_type=jnp.float32,
    )
    value, gate = projt[:units], projt[units:]
    cdf = 0.5 * (1.0 + lax.erf(gate * 2.0 ** (-0.5)))
    density = jnp.exp(-0.5 * gate * gate) * (2.0 * jnp.pi) ** (-0.5)
    actt = (value * gate * cdf).astype(jnp.bfloat16)
    dactt = lax.dot_general(
        w_out_c, both_cot, (((1,), (1,)), ((), ())), preferred_element_type=jnp.float32
    )
    d_value = dactt * gate * cdf
    d_gate = dactt * value * (cdf + gate * density)
    dprojt = jnp.concatenate([d_value, d_gate], axis=0).astype(jnp.bfloat16)

    grad_in, grad_out, grad_normed = sum_all(
        n, factor, dprojt.reshape(n, gi, 2 * tokens), both,
        both_cot.T.reshape(n, go, 2 * tokens), actt, w_in_c,
    )
    return (grad_in.reshape(2 * gi, model), grad_out, grad_normed)


def solution(mesh):
    placed = (P(("grp", "dp"), None), P(), P(), P(("grp", "dp"), None))
    return jax.shard_map(
        local,
        mesh=mesh,
        in_specs=placed,
        out_specs=(P("dp", None), P("dp", None), P(("grp", "dp"), None)),
        check_vma=False,
    )
```

```python
import functools

import jax
import jax.numpy as jnp
from jax import lax
from jax.experimental import pallas as pl
from jax.experimental.pallas import tpu as pltpu
from jax.sharding import PartitionSpec as P

MESH = pl.DeviceIdType.MESH


def greet(partners):
    barrier = pltpu.get_barrier_semaphore()
    for partner in partners:
        pl.semaphore_signal(barrier, inc=1, device_id=partner, device_id_type=MESH)
    pl.semaphore_wait(barrier, len(partners))


def head_kernel(
    n, normed, cot, w_out, w_in, all_normed, cott, dprojt, actt,
    mine, theirs, w_now, w_outt, send_sem, recv_sem, fetch,
):
    grp = lax.axis_index("grp")
    dp = lax.axis_index("dp")
    core = lax.rem(grp, 2)
    other = (grp + 1 - 2 * core, dp)
    rows, model = normed.shape
    gi, go = dprojt.shape[1], cott.shape[1]
    half = n // 2
    loads = [
        pltpu.make_async_copy(w_in.at[d, core], w_now.at[d], fetch.at[d]) for d in range(n)
    ]
    for load in loads:
        load.start()
    mine[0] = cot[...].astype(jnp.float32)
    mine[1] = normed[...].astype(jnp.float32)
    greet([other])
    copies = [
        pltpu.make_async_remote_copy(
            src_ref=mine.at[k], dst_ref=theirs.at[k], send_sem=send_sem.at[k],
            recv_sem=recv_sem.at[k], device_id=other, device_id_type=MESH,
        )
        for k in range(2)
    ]
    for copy in copies:
        copy.start()
    step = w_out.shape[1] // 4
    for j in range(4):
        part = slice(j * step, (j + 1) * step)
        w_outt[part, :] = w_out[:, part].T
    all_normed[:rows] = normed[...]
    turned = cot[...].T
    for d in range(n):
        cott[d, :, :rows] = turned[d * go : (d + 1) * go]
    copies[0].wait_recv()
    turned = theirs[0].T.astype(jnp.bfloat16)
    for d in range(n):
        cott[d, :, rows:] = turned[d * go : (d + 1) * go]
    copies[1].wait_recv()
    all_normed[rows:] = theirs[1].astype(jnp.bfloat16)
    for load in loads:
        load.wait()

    def dot(left, right, axis):
        return lax.dot_general(
            left, right, (((1,), (axis,)), ((), ())), preferred_element_type=jnp.float32
        )

    tokens_t = cott[...].reshape(model, 2 * rows)

    def block(b, carry):
        value = dot(w_now[b], all_normed[...], 1)
        gate = dot(w_now[b + half], all_normed[...], 1)
        units = pl.ds(pl.multiple_of((2 * b + core) * gi, 16), gi)
        dact = dot(w_outt[units, :], tokens_t, 0)
        cdf = 0.5 * (1.0 + lax.erf(gate * 2.0 ** (-0.5)))
        density = jnp.exp(-0.5 * gate * gate) * (2.0 * jnp.pi) ** (-0.5)
        gelu = gate * cdf
        actt[pl.ds(pl.multiple_of(b * gi, 16), gi), :] = (value * gelu).astype(jnp.bfloat16)
        dprojt[b] = (dact * gelu).astype(jnp.bfloat16)
        dprojt[b + half] = (dact * value * (cdf + gate * density)).astype(jnp.bfloat16)
        return carry

    lax.fori_loop(0, half, block, 0)
    for copy in copies:
        copy.wait_send()


def make_terms(n, normed, cot, w_out, w_in):
    rows, model = normed.shape
    gi, width = w_in.shape[2], w_out.shape[1]
    go = model // n
    bf16 = jnp.bfloat16
    vmem = pl.BlockSpec(memory_space=pltpu.VMEM)
    return pl.pallas_call(
        functools.partial(head_kernel, n),
        out_shape=(
            jax.ShapeDtypeStruct((2 * rows, model), bf16),
            jax.ShapeDtypeStruct((n, go, 2 * rows), bf16),
            jax.ShapeDtypeStruct((n, gi, 2 * rows), bf16),
            jax.ShapeDtypeStruct((width // 2, 2 * rows), bf16),
        ),
        in_specs=[vmem] * 3 + [pl.BlockSpec(memory_space=pl.ANY)],
        out_specs=(vmem,) * 4,
        scratch_shapes=[
            pltpu.VMEM((2, rows, model), jnp.float32),
            pltpu.VMEM((2, rows, model), jnp.float32),
            pltpu.VMEM((n, gi, model), bf16),
            pltpu.VMEM((width, model), bf16),
            pltpu.SemaphoreType.DMA((2,)),
            pltpu.SemaphoreType.DMA((2,)),
            pltpu.SemaphoreType.DMA((n,)),
        ],
        compiler_params=pltpu.CompilerParams(
            collective_id=0, has_side_effects=True, vmem_limit_bytes=60 * 2**20
        ),
        name="make_terms",
    )(normed, cot, w_out, w_in)


def sum_kernel(
    n, factor, dprojt, normed, cott, actt, w_in, out_in, out_out, out_normed,
    part_r, part_e, land_r, land_e, land_x, final_r, land_p, land_o, share, land_s, w_now,
    ring_r, ring_x, halves, pair_r, core_r, core_o, spread, core_s, fetch,
):
    grp = lax.axis_index("grp")
    dp = lax.axis_index("dp")
    x, core = grp // 2, lax.rem(grp, 2)
    half = n // 2
    up = lax.rem(dp, 2)
    pos = jnp.where(up == 0, dp // 2, n - 1 - dp // 2)

    def member(place):
        place = lax.rem(place + 2 * n, n)
        return jnp.where(place < half, 2 * place, 2 * (n - 1 - place) + 1)

    following, previous = (grp, member(pos + 1)), (grp, member(pos - 1))
    along_x = ((1 - x) * 2 + core, dp)
    other = (x * 2 + 1 - core, dp)
    greet([following, previous, along_x, other])
    onward = (following, previous)

    gi, go = dprojt.shape[1], cott.shape[1]
    rows_r = part_r.shape[1]
    rows_h, cols = land_e.shape[2:]
    split = rows_r - go
    spans = (slice(0, cols), slice(cols, 2 * cols))

    def dot(left, right, axes):
        return lax.dot_general(
            left, right, (((axes[0],), (axes[1],)), ((), ())),
            preferred_element_type=jnp.float32,
        )

    def owner(way, s):
        return member(pos - 1 - s) if way == 0 else member(pos + 1 + s)

    def compute_r(way, s):
        d = owner(way, s)
        part_r[way, :go] = dot(cott[d], actt[spans[way], :], (1, 1))
        part_r[way, go:] = dot(dprojt[d, :split], normed[:, spans[way]], (1, 0))

    def rows_of_half(h):
        return pl.ds(pl.multiple_of(split + h * rows_h, 16), rows_h)

    def compute_x(way, s, h):
        d = owner(way, s)
        return dot(dprojt[d, rows_of_half(h)], normed[:, spans[way]], (1, 0))

    def remote(src, dst, sems, where, device):
        return pltpu.make_async_remote_copy(
            src_ref=src, dst_ref=dst, send_sem=sems.at[(0,) + where],
            recv_sem=sems.at[(1,) + where], device_id=device, device_id_type=MESH,
        )

    def hop_r(way, s, first=False):
        src = final_r.at[way] if first else land_r.at[way, s - 1]
        return remote(src, land_r.at[way, s], ring_r, (way, s), onward[way])

    def hop_x(way, s, first=False):
        src = land_e.at[0, way] if first else land_x.at[way, s - 1]
        return remote(src, land_x.at[way, s], ring_x, (way, s), onward[way])

    def give_half(s):
        return remote(part_e.at[s], land_e.at[s], halves, (s,), along_x)

    def loop(first, last, body):
        def step(s, carry):
            body(s)
            return carry

        lax.fori_loop(first, last, step, 0)

    for way in range(2):
        compute_r(way, 0)
        final_r[way] = part_r[way]
        hop_r(way, 0, True).start()

    def make_x(s):
        for way in range(2):
            part_e[s, way] = compute_x(way, s, 1 - x)
        give_half(s).start()

    loop(0, n, make_x)

    tokens = out_normed.shape[0]

    def add_share(d, k, total):
        copy = pltpu.make_async_copy(w_in.at[d, core], w_now, fetch)
        copy.start()
        copy.wait()
        rows = slice(k * tokens, (k + 1) * tokens)
        for span in spans:
            total[:, span] += dot(dprojt[d, :, rows], w_now[:, span], (0, 0))

    share[...] = jnp.zeros_like(share)
    loop(0, n, lambda d: add_share(d, 1, share))
    give_share = remote(share, land_s, core_s, (), other)
    give_share.start()

    def step_r(s):
        for way in range(2):
            compute_r(way, s + 1)
        for way in range(2):
            hop_r(way, s, True).wait_recv()
            land_r[way, s] = land_r[way, s] + part_r[way]
            hop_r(way, s + 1).start()

    def step_first(s):
        step_r(s)
        add_share(s, 0, land_s)

    def own_x(way, s):
        return compute_x(way, s, x) + land_e[s, way]

    def step_x(s):
        give_half(s + 1).wait_recv()
        for way in range(2):
            land_e[s + 1, way] = own_x(way, s + 1)
        for way in range(2):
            hop_x(way, s, True).wait_recv()
            land_x[way, s] = land_x[way, s] + land_e[s + 1, way]
            hop_x(way, s + 1).start()

    def step_both(s):
        step_r(s)
        step_x(s - lag)
        add_share(s, 0, land_s)

    lag = min(n // 2, n - 2)
    step_r(0)
    give_share.wait_recv()
    for d in (0, n - 2, n - 1):
        add_share(d, 0, land_s)
    loop(1, lag, step_first)
    give_half(0).wait_recv()
    for way in range(2):
        land_e[0, way] = own_x(way, 0)
        hop_x(way, 0, True).start()
    loop(lag, n - 2, step_both)

    out_normed[...] = land_s[...].astype(out_normed.dtype)

    def swap_r(way):
        return remote(part_r.at[way], land_p.at[way], pair_r, (way,), along_x)

    for way in range(2):
        compute_r(way, n - 1)
        hop_r(way, n - 2, True).wait_recv()
        part_r[way] = (land_r[way, n - 2] + part_r[way]) * factor
        swap_r(way).start()

    loop(n - 2 - lag, n - 2, step_x)

    def tell_r(c, way):
        spot = out_in.at[c, :split, spans[way]]
        return remote(spot, spot, core_r, (way,), other)

    def tell_o(way):
        return remote(final_r.at[way, :go], land_o.at[way], core_o, (way,), other)

    def show(which, c, h, way, device):
        rows = pl.ds(pl.multiple_of(split + h * rows_h, 8), rows_h)
        spot = out_in.at[c, rows, spans[way]]
        return remote(spot, spot, spread, (which, way), device)

    give_half(n - 1).wait_recv()
    for way in range(2):
        land_e[n - 1, way] = own_x(way, n - 1)
    rows_x = pl.ds(pl.multiple_of(split + x * rows_h, 8), rows_h)
    for way in range(2):
        hop_x(way, n - 2, True).wait_recv()
        out_in[core, rows_x, spans[way]] = (
            land_x[way, n - 2] + land_e[n - 1, way]
        ) * factor
        show(0, core, x, way, along_x).start()
        show(1, core, x, way, other).start()
    for way in range(2):
        swap_r(way).wait_recv()
        hop_r(way, 0, True).wait_send()
        final_r[way, :go] = part_r[way, :go] + land_p[way, :go]
        tell_o(way).start()
        out_in[core, :split, spans[way]] = part_r[way, go:] + land_p[way, go:]
        tell_r(core, way).start()
    for way in range(2):
        show(0, core, 1 - x, way, along_x).wait_recv()
        show(2, core, 1 - x, way, other).start()
    for way in range(2):
        tell_o(way).wait_recv()
    mine = jnp.concatenate([final_r[0, :go], final_r[1, :go]], axis=1)
    theirs = jnp.concatenate([land_o[0], land_o[1]], axis=1)
    first = jnp.where(core == 0, mine, theirs)
    second = jnp.where(core == 0, theirs, mine)
    out_out[...] = jnp.concatenate(
        [
            block[:, b * gi : (b + 1) * gi]
            for b in range(half)
            for block in (first, second)
        ],
        axis=1,
    )
    for way in range(2):
        tell_r(1 - core, way).wait_recv()
        show(1, 1 - core, x, way, other).wait_recv()
        show(2, 1 - core, 1 - x, way, other).wait_recv()

    def drain(s):
        for way in range(2):
            hop_r(way, s + 1).wait_send()
            hop_x(way, s, True).wait_send()

    loop(0, n - 2, drain)
    for way in range(2):
        hop_x(way, n - 2, True).wait_send()
    loop(0, n, lambda s: give_half(s).wait_send())
    give_share.wait_send()
    for way in range(2):
        swap_r(way).wait_send()
        tell_o(way).wait_send()
        tell_r(core, way).wait_send()
        show(0, core, x, way, along_x).wait_send()
        show(1, core, x, way, other).wait_send()
        show(2, core, 1 - x, way, other).wait_send()


def sum_all(n, factor, dprojt, normed, cott, actt, w_in):
    gi, go, width = dprojt.shape[1], cott.shape[1], normed.shape[1]
    units = actt.shape[0]
    rows = gi + go
    rows_x = rows * 7 // 15 // 32 * 32
    rows_r, rows_h, cols = rows - rows_x, rows_x // 2, width // 2
    vmem = pl.BlockSpec(memory_space=pltpu.VMEM)
    f32 = jnp.float32
    dma = pltpu.SemaphoreType.DMA
    tokens = normed.shape[0] // 2
    return pl.pallas_call(
        functools.partial(sum_kernel, n, factor),
        out_shape=(
            jax.ShapeDtypeStruct((2, gi, width), f32),
            jax.ShapeDtypeStruct((go, 2 * units), f32),
            jax.ShapeDtypeStruct((tokens, width), jnp.bfloat16),
        ),
        in_specs=[vmem] * 4 + [pl.BlockSpec(memory_space=pl.ANY)],
        out_specs=(vmem,) * 3,
        scratch_shapes=[
            pltpu.VMEM((2, rows_r, cols), f32),
            pltpu.VMEM((n, 2, rows_h, cols), f32),
            pltpu.VMEM((2, n - 1, rows_r, cols), f32),
            pltpu.VMEM((n, 2, rows_h, cols), f32),
            pltpu.VMEM((2, n - 1, rows_h, cols), f32),
            pltpu.VMEM((2, rows_r, cols), f32),
            pltpu.VMEM((2, rows_r, cols), f32),
            pltpu.VMEM((2, go, cols), f32),
            pltpu.VMEM((tokens, width), f32),
            pltpu.VMEM((tokens, width), f32),
            pltpu.VMEM((gi, width), jnp.bfloat16),
            dma((2, 2, n - 1)),
            dma((2, 2, n - 1)),
            dma((2, n)),
            dma((2, 2)),
            dma((2, 2)),
            dma((2, 2)),
            dma((2, 3, 2)),
            dma((2,)),
            dma,
        ],
        compiler_params=pltpu.CompilerParams(
            collective_id=1, has_side_effects=True, vmem_limit_bytes=62 * 2**20
        ),
        cost_estimate=pl.CostEstimate(
            flops=6 * n * rows * tokens * width, bytes_accessed=20 * 2**20, transcendentals=0
        ),
        name="sum_gradients",
    )(dprojt, normed, cott, actt, w_in)


def local(normed, w_in, w_out, cotangent):
    width = w_out.shape[1]
    model = w_in.shape[1]
    n = lax.axis_size("dp")
    outer = lax.axis_size("grp")
    tokens = normed.shape[0]
    factor = (tokens * n * outer) ** (-0.5)
    gi = width // n
    blocks = w_in.reshape(n, 2, gi, model)
    both, cott, dprojt, actt = make_terms(n, normed, cotangent, w_out, blocks)
    grad_in, grad_out, grad_normed = sum_all(n, factor, dprojt, both, cott, actt, blocks)
    return (grad_in.reshape(2 * gi, model), grad_out, grad_normed)


def solution(mesh):
    placed = (P(("grp", "dp"), None), P(), P(), P(("grp", "dp"), None))
    return jax.shard_map(
        local,
        mesh=mesh,
        in_specs=placed,
        out_specs=(P("dp", None), P("dp", None), P(("grp", "dp"), None)),
        check_vma=False,
    )
```

```python
import functools

import jax
import jax.numpy as jnp
from jax import lax
from jax.experimental import pallas as pl
from jax.experimental.pallas import tpu as pltpu
from jax.sharding import PartitionSpec as P

MESH = pl.DeviceIdType.MESH


def greet(partners):
    barrier = pltpu.get_barrier_semaphore()
    for partner in partners:
        pl.semaphore_signal(barrier, inc=1, device_id=partner, device_id_type=MESH)
    pl.semaphore_wait(barrier, len(partners))


def head_kernel(
    n, normed, cot, w_out, w_in, all_normed, cott, dprojt, actt,
    mine, theirs, w_now, w_outt, send_sem, recv_sem, fetch,
):
    grp = lax.axis_index("grp")
    dp = lax.axis_index("dp")
    core = lax.rem(grp, 2)
    other = (grp + 1 - 2 * core, dp)
    rows, model = normed.shape
    gi, go = dprojt.shape[1], cott.shape[1]
    half = n // 2
    loads = [
        pltpu.make_async_copy(w_in.at[d, core], w_now.at[d], fetch.at[d]) for d in range(n)
    ]
    for load in loads:
        load.start()
    mine[0] = cot[...].astype(jnp.float32)
    mine[1] = normed[...].astype(jnp.float32)
    greet([other])
    copies = [
        pltpu.make_async_remote_copy(
            src_ref=mine.at[k], dst_ref=theirs.at[k], send_sem=send_sem.at[k],
            recv_sem=recv_sem.at[k], device_id=other, device_id_type=MESH,
        )
        for k in range(2)
    ]
    for copy in copies:
        copy.start()
    step = w_out.shape[1] // 4
    for j in range(4):
        part = slice(j * step, (j + 1) * step)
        w_outt[part, :] = w_out[:, part].T
    all_normed[:rows] = normed[...]
    turned = cot[...].T
    for d in range(n):
        cott[d, :, :rows] = turned[d * go : (d + 1) * go]
    copies[0].wait_recv()
    turned = theirs[0].T.astype(jnp.bfloat16)
    for d in range(n):
        cott[d, :, rows:] = turned[d * go : (d + 1) * go]
    copies[1].wait_recv()
    all_normed[rows:] = theirs[1].astype(jnp.bfloat16)
    for load in loads:
        load.wait()

    def dot(left, right, axis):
        return lax.dot_general(
            left, right, (((1,), (axis,)), ((), ())), preferred_element_type=jnp.float32
        )

    tokens_t = cott[...].reshape(model, 2 * rows)

    def block(b, carry):
        value = dot(w_now[b], all_normed[...], 1)
        gate = dot(w_now[b + half], all_normed[...], 1)
        units = pl.ds(pl.multiple_of((2 * b + core) * gi, 16), gi)
        dact = dot(w_outt[units, :], tokens_t, 0)
        cdf = 0.5 * (1.0 + lax.erf(gate * 2.0 ** (-0.5)))
        density = jnp.exp(-0.5 * gate * gate) * (2.0 * jnp.pi) ** (-0.5)
        gelu = gate * cdf
        actt[pl.ds(pl.multiple_of(b * gi, 16), gi), :] = (value * gelu).astype(jnp.bfloat16)
        dprojt[b] = (dact * gelu).astype(jnp.bfloat16)
        dprojt[b + half] = (dact * value * (cdf + gate * density)).astype(jnp.bfloat16)
        return carry

    lax.fori_loop(0, half, block, 0)
    for copy in copies:
        copy.wait_send()


def make_terms(n, normed, cot, w_out, w_in):
    rows, model = normed.shape
    gi, width = w_in.shape[2], w_out.shape[1]
    go = model // n
    bf16 = jnp.bfloat16
    vmem = pl.BlockSpec(memory_space=pltpu.VMEM)
    return pl.pallas_call(
        functools.partial(head_kernel, n),
        out_shape=(
            jax.ShapeDtypeStruct((2 * rows, model), bf16),
            jax.ShapeDtypeStruct((n, go, 2 * rows), bf16),
            jax.ShapeDtypeStruct((n, gi, 2 * rows), bf16),
            jax.ShapeDtypeStruct((width // 2, 2 * rows), bf16),
        ),
        in_specs=[vmem] * 3 + [pl.BlockSpec(memory_space=pl.ANY)],
        out_specs=(vmem,) * 4,
        scratch_shapes=[
            pltpu.VMEM((2, rows, model), jnp.float32),
            pltpu.VMEM((2, rows, model), jnp.float32),
            pltpu.VMEM((n, gi, model), bf16),
            pltpu.VMEM((width, model), bf16),
            pltpu.SemaphoreType.DMA((2,)),
            pltpu.SemaphoreType.DMA((2,)),
            pltpu.SemaphoreType.DMA((n,)),
        ],
        compiler_params=pltpu.CompilerParams(
            collective_id=0, has_side_effects=True, vmem_limit_bytes=60 * 2**20
        ),
        name="make_terms",
    )(normed, cot, w_out, w_in)


def sum_kernel(
    n, factor, dprojt, normed, cott, actt, w_in, out_in, out_out, out_normed,
    part_r, part_e, land_r, land_e, land_x, final_r, land_p, land_o, share, land_s, w_now,
    ring_r, ring_x, halves, pair_r, core_r, core_o, spread, core_s, fetch,
):
    grp = lax.axis_index("grp")
    dp = lax.axis_index("dp")
    x, core = grp // 2, lax.rem(grp, 2)
    half = n // 2
    up = lax.rem(dp, 2)
    pos = jnp.where(up == 0, dp // 2, n - 1 - dp // 2)

    def member(place):
        place = lax.rem(place + 2 * n, n)
        return jnp.where(place < half, 2 * place, 2 * (n - 1 - place) + 1)

    following, previous = (grp, member(pos + 1)), (grp, member(pos - 1))
    along_x = ((1 - x) * 2 + core, dp)
    other = (x * 2 + 1 - core, dp)
    greet([following, previous, along_x, other])
    onward = (following, previous)

    gi, go = dprojt.shape[1], cott.shape[1]
    rows_r = part_r.shape[1]
    rows_h, cols = land_e.shape[2:]
    split = rows_r - go
    spans = (slice(0, cols), slice(cols, 2 * cols))

    def dot(left, right, axes):
        return lax.dot_general(
            left, right, (((axes[0],), (axes[1],)), ((), ())),
            preferred_element_type=jnp.float32,
        )

    def owner(way, s):
        return member(pos - 1 - s) if way == 0 else member(pos + 1 + s)

    def compute_r(way, s):
        d = owner(way, s)
        part_r[way, :go] = dot(cott[d], actt[spans[way], :], (1, 1))
        part_r[way, go:] = dot(dprojt[d, :split], normed[:, spans[way]], (1, 0))

    def rows_of_half(h):
        return pl.ds(pl.multiple_of(split + h * rows_h, 16), rows_h)

    def compute_x(way, s, h):
        d = owner(way, s)
        return dot(dprojt[d, rows_of_half(h)], normed[:, spans[way]], (1, 0))

    def remote(src, dst, sems, where, device):
        return pltpu.make_async_remote_copy(
            src_ref=src, dst_ref=dst, send_sem=sems.at[(0,) + where],
            recv_sem=sems.at[(1,) + where], device_id=device, device_id_type=MESH,
        )

    streams = [(way, k) for k in range(2) for way in range(2)]
    cut_r, cut_x = rows_r // 16 * 8, rows_h // 16 * 8
    group_r = (slice(0, cut_r), slice(cut_r, rows_r))
    group_x = (slice(0, cut_x), slice(cut_x, rows_h))

    def hop_r(way, k, s, first=False):
        rows = group_r[k]
        src = final_r.at[way, rows] if first else land_r.at[way, s - 1, rows]
        return remote(src, land_r.at[way, s, rows], ring_r, (2 * way + k, s), onward[way])

    def hop_x(way, k, s, first=False):
        rows = group_x[k]
        src = land_e.at[0, way, rows] if first else land_x.at[way, s - 1, rows]
        return remote(src, land_x.at[way, s, rows], ring_x, (2 * way + k, s), onward[way])

    def give_half(s):
        return remote(part_e.at[s], land_e.at[s], halves, (s,), along_x)

    def loop(first, last, body):
        def step(s, carry):
            body(s)
            return carry

        lax.fori_loop(first, last, step, 0)

    for way in range(2):
        compute_r(way, 0)
        final_r[way] = part_r[way]
    for way, k in streams:
        hop_r(way, k, 0, True).start()

    def make_x(s):
        for way in range(2):
            part_e[s, way] = compute_x(way, s, 1 - x)
        give_half(s).start()

    loop(0, n, make_x)

    tokens = out_normed.shape[0]

    def add_share(d, k, total):
        copy = pltpu.make_async_copy(w_in.at[d, core], w_now, fetch)
        copy.start()
        copy.wait()
        rows = slice(k * tokens, (k + 1) * tokens)
        for span in spans:
            total[:, span] += dot(dprojt[d, :, rows], w_now[:, span], (0, 0))

    share[...] = jnp.zeros_like(share)
    loop(0, n, lambda d: add_share(d, 1, share))
    give_share = remote(share, land_s, core_s, (), other)
    give_share.start()

    def step_r(s):
        for way in range(2):
            compute_r(way, s + 1)
        for way, k in streams:
            hop_r(way, k, s, True).wait_recv()
            rows = group_r[k]
            land_r[way, s, rows] = land_r[way, s, rows] + part_r[way, rows]
            hop_r(way, k, s + 1).start()

    def step_first(s):
        step_r(s)
        add_share(s, 0, land_s)

    def own_x(way, s):
        return compute_x(way, s, x) + land_e[s, way]

    def step_x(s):
        give_half(s + 1).wait_recv()
        for way in range(2):
            land_e[s + 1, way] = own_x(way, s + 1)
        for way, k in streams:
            hop_x(way, k, s, True).wait_recv()
            rows = group_x[k]
            land_x[way, s, rows] = land_x[way, s, rows] + land_e[s + 1, way, rows]
            hop_x(way, k, s + 1).start()

    def step_both(s):
        step_r(s)
        step_x(s - lag)
        add_share(s, 0, land_s)

    lag = min(n // 2, n - 2)
    step_r(0)
    give_share.wait_recv()
    for d in (0, n - 2, n - 1):
        add_share(d, 0, land_s)
    loop(1, lag, step_first)
    give_half(0).wait_recv()
    for way in range(2):
        land_e[0, way] = own_x(way, 0)
    for way, k in streams:
        hop_x(way, k, 0, True).start()
    loop(lag, n - 2, step_both)

    out_normed[...] = land_s[...].astype(out_normed.dtype)

    def swap_r(way):
        return remote(part_r.at[way], land_p.at[way], pair_r, (way,), along_x)

    for way in range(2):
        compute_r(way, n - 1)
        for k in range(2):
            hop_r(way, k, n - 2, True).wait_recv()
        part_r[way] = (land_r[way, n - 2] + part_r[way]) * factor
        swap_r(way).start()

    loop(n - 2 - lag, n - 2, step_x)

    def tell_r(c, way):
        spot = out_in.at[c, :split, spans[way]]
        return remote(spot, spot, core_r, (way,), other)

    def tell_o(way):
        return remote(final_r.at[way, :go], land_o.at[way], core_o, (way,), other)

    def x_rows(h, k):
        start = split + h * rows_h + group_x[k].start
        return pl.ds(pl.multiple_of(start, 8), group_x[k].stop - group_x[k].start)

    def show(which, c, h, way, k, device):
        spot = out_in.at[c, x_rows(h, k), spans[way]]
        return remote(spot, spot, spread, (which, 2 * way + k), device)

    give_half(n - 1).wait_recv()
    for way in range(2):
        land_e[n - 1, way] = own_x(way, n - 1)
    for way, k in streams:
        hop_x(way, k, n - 2, True).wait_recv()
        rows = group_x[k]
        out_in[core, x_rows(x, k), spans[way]] = (
            land_x[way, n - 2, rows] + land_e[n - 1, way, rows]
        ) * factor
        show(0, core, x, way, k, along_x).start()
        show(1, core, x, way, k, other).start()
    for way in range(2):
        swap_r(way).wait_recv()
        for k in range(2):
            hop_r(way, k, 0, True).wait_send()
        final_r[way, :go] = part_r[way, :go] + land_p[way, :go]
        tell_o(way).start()
        out_in[core, :split, spans[way]] = part_r[way, go:] + land_p[way, go:]
        tell_r(core, way).start()
    for way, k in streams:
        show(0, core, 1 - x, way, k, along_x).wait_recv()
        show(2, core, 1 - x, way, k, other).start()
    for way in range(2):
        tell_o(way).wait_recv()
    mine = jnp.concatenate([final_r[0, :go], final_r[1, :go]], axis=1)
    theirs = jnp.concatenate([land_o[0], land_o[1]], axis=1)
    first = jnp.where(core == 0, mine, theirs)
    second = jnp.where(core == 0, theirs, mine)
    out_out[...] = jnp.concatenate(
        [
            block[:, b * gi : (b + 1) * gi]
            for b in range(half)
            for block in (first, second)
        ],
        axis=1,
    )
    for way in range(2):
        tell_r(1 - core, way).wait_recv()
    for way, k in streams:
        show(1, 1 - core, x, way, k, other).wait_recv()
        show(2, 1 - core, 1 - x, way, k, other).wait_recv()

    def drain(s):
        for way, k in streams:
            hop_r(way, k, s + 1).wait_send()
            hop_x(way, k, s, True).wait_send()

    loop(0, n - 2, drain)
    for way, k in streams:
        hop_x(way, k, n - 2, True).wait_send()
    loop(0, n, lambda s: give_half(s).wait_send())
    give_share.wait_send()
    for way in range(2):
        swap_r(way).wait_send()
        tell_o(way).wait_send()
        tell_r(core, way).wait_send()
    for way, k in streams:
        show(0, core, x, way, k, along_x).wait_send()
        show(1, core, x, way, k, other).wait_send()
        show(2, core, 1 - x, way, k, other).wait_send()


def sum_all(n, factor, dprojt, normed, cott, actt, w_in):
    gi, go, width = dprojt.shape[1], cott.shape[1], normed.shape[1]
    units = actt.shape[0]
    rows = gi + go
    rows_x = rows * 7 // 15 // 32 * 32
    rows_r, rows_h, cols = rows - rows_x, rows_x // 2, width // 2
    vmem = pl.BlockSpec(memory_space=pltpu.VMEM)
    f32 = jnp.float32
    dma = pltpu.SemaphoreType.DMA
    tokens = normed.shape[0] // 2
    return pl.pallas_call(
        functools.partial(sum_kernel, n, factor),
        out_shape=(
            jax.ShapeDtypeStruct((2, gi, width), f32),
            jax.ShapeDtypeStruct((go, 2 * units), f32),
            jax.ShapeDtypeStruct((tokens, width), jnp.bfloat16),
        ),
        in_specs=[vmem] * 4 + [pl.BlockSpec(memory_space=pl.ANY)],
        out_specs=(vmem,) * 3,
        scratch_shapes=[
            pltpu.VMEM((2, rows_r, cols), f32),
            pltpu.VMEM((n, 2, rows_h, cols), f32),
            pltpu.VMEM((2, n - 1, rows_r, cols), f32),
            pltpu.VMEM((n, 2, rows_h, cols), f32),
            pltpu.VMEM((2, n - 1, rows_h, cols), f32),
            pltpu.VMEM((2, rows_r, cols), f32),
            pltpu.VMEM((2, rows_r, cols), f32),
            pltpu.VMEM((2, go, cols), f32),
            pltpu.VMEM((tokens, width), f32),
            pltpu.VMEM((tokens, width), f32),
            pltpu.VMEM((gi, width), jnp.bfloat16),
            dma((2, 4, n - 1)),
            dma((2, 4, n - 1)),
            dma((2, n)),
            dma((2, 2)),
            dma((2, 2)),
            dma((2, 2)),
            dma((2, 3, 4)),
            dma((2,)),
            dma,
        ],
        compiler_params=pltpu.CompilerParams(
            collective_id=1, has_side_effects=True, vmem_limit_bytes=62 * 2**20
        ),
        cost_estimate=pl.CostEstimate(
            flops=6 * n * rows * tokens * width, bytes_accessed=20 * 2**20, transcendentals=0
        ),
        name="sum_gradients",
    )(dprojt, normed, cott, actt, w_in)


def local(normed, w_in, w_out, cotangent):
    width = w_out.shape[1]
    model = w_in.shape[1]
    n = lax.axis_size("dp")
    outer = lax.axis_size("grp")
    tokens = normed.shape[0]
    factor = (tokens * n * outer) ** (-0.5)
    gi = width // n
    blocks = w_in.reshape(n, 2, gi, model)
    both, cott, dprojt, actt = make_terms(n, normed, cotangent, w_out, blocks)
    grad_in, grad_out, grad_normed = sum_all(n, factor, dprojt, both, cott, actt, blocks)
    return (grad_in.reshape(2 * gi, model), grad_out, grad_normed)


def solution(mesh):
    placed = (P(("grp", "dp"), None), P(), P(), P(("grp", "dp"), None))
    return jax.shard_map(
        local,
        mesh=mesh,
        in_specs=placed,
        out_specs=(P("dp", None), P("dp", None), P(("grp", "dp"), None)),
        check_vma=False,
    )
```

```python
import functools

import jax
import jax.numpy as jnp
from jax import lax
from jax.experimental import pallas as pl
from jax.experimental.pallas import tpu as pltpu
from jax.sharding import PartitionSpec as P

MESH = pl.DeviceIdType.MESH


def greet(partners):
    barrier = pltpu.get_barrier_semaphore()
    for partner in partners:
        pl.semaphore_signal(barrier, inc=1, device_id=partner, device_id_type=MESH)
    pl.semaphore_wait(barrier, len(partners))


def head_kernel(
    n, normed, cot, w_out, w_in, all_normed, cott, dprojt, actt,
    mine, theirs, w_now, w_outt, send_sem, recv_sem, fetch,
):
    grp = lax.axis_index("grp")
    dp = lax.axis_index("dp")
    core = lax.rem(grp, 2)
    other = (grp + 1 - 2 * core, dp)
    rows, model = normed.shape
    gi, go = dprojt.shape[1], cott.shape[1]
    half = n // 2
    loads = [
        pltpu.make_async_copy(w_in.at[d, core], w_now.at[d], fetch.at[d]) for d in range(n)
    ]
    for load in loads:
        load.start()
    mine[0] = cot[...].astype(jnp.float32)
    mine[1] = normed[...].astype(jnp.float32)
    greet([other])
    copies = [
        pltpu.make_async_remote_copy(
            src_ref=mine.at[k], dst_ref=theirs.at[k], send_sem=send_sem.at[k],
            recv_sem=recv_sem.at[k], device_id=other, device_id_type=MESH,
        )
        for k in range(2)
    ]
    for copy in copies:
        copy.start()
    step = w_out.shape[1] // 4
    for j in range(4):
        part = slice(j * step, (j + 1) * step)
        w_outt[part, :] = w_out[:, part].T
    all_normed[:rows] = normed[...]
    turned = cot[...].T
    for d in range(n):
        cott[d, :, :rows] = turned[d * go : (d + 1) * go]
    copies[0].wait_recv()
    turned = theirs[0].T.astype(jnp.bfloat16)
    for d in range(n):
        cott[d, :, rows:] = turned[d * go : (d + 1) * go]
    copies[1].wait_recv()
    all_normed[rows:] = theirs[1].astype(jnp.bfloat16)
    for load in loads:
        load.wait()

    def dot(left, right, axis):
        return lax.dot_general(
            left, right, (((1,), (axis,)), ((), ())), preferred_element_type=jnp.float32
        )

    tokens_t = cott[...].reshape(model, 2 * rows)

    def block(b, carry):
        value = dot(w_now[b], all_normed[...], 1)
        gate = dot(w_now[b + half], all_normed[...], 1)
        units = pl.ds(pl.multiple_of((2 * b + core) * gi, 16), gi)
        dact = dot(w_outt[units, :], tokens_t, 0)
        cdf = 0.5 * (1.0 + lax.erf(gate * 2.0 ** (-0.5)))
        density = jnp.exp(-0.5 * gate * gate) * (2.0 * jnp.pi) ** (-0.5)
        gelu = gate * cdf
        actt[pl.ds(pl.multiple_of(b * gi, 16), gi), :] = (value * gelu).astype(jnp.bfloat16)
        dprojt[b] = (dact * gelu).astype(jnp.bfloat16)
        dprojt[b + half] = (dact * value * (cdf + gate * density)).astype(jnp.bfloat16)
        return carry

    lax.fori_loop(0, half, block, 0)
    for copy in copies:
        copy.wait_send()


def make_terms(n, normed, cot, w_out, w_in):
    rows, model = normed.shape
    gi, width = w_in.shape[2], w_out.shape[1]
    go = model // n
    bf16 = jnp.bfloat16
    vmem = pl.BlockSpec(memory_space=pltpu.VMEM)
    return pl.pallas_call(
        functools.partial(head_kernel, n),
        out_shape=(
            jax.ShapeDtypeStruct((2 * rows, model), bf16),
            jax.ShapeDtypeStruct((n, go, 2 * rows), bf16),
            jax.ShapeDtypeStruct((n, gi, 2 * rows), bf16),
            jax.ShapeDtypeStruct((width // 2, 2 * rows), bf16),
        ),
        in_specs=[vmem] * 3 + [pl.BlockSpec(memory_space=pl.ANY)],
        out_specs=(vmem,) * 4,
        scratch_shapes=[
            pltpu.VMEM((2, rows, model), jnp.float32),
            pltpu.VMEM((2, rows, model), jnp.float32),
            pltpu.VMEM((n, gi, model), bf16),
            pltpu.VMEM((width, model), bf16),
            pltpu.SemaphoreType.DMA((2,)),
            pltpu.SemaphoreType.DMA((2,)),
            pltpu.SemaphoreType.DMA((n,)),
        ],
        compiler_params=pltpu.CompilerParams(
            collective_id=0, has_side_effects=True, vmem_limit_bytes=60 * 2**20
        ),
        name="make_terms",
    )(normed, cot, w_out, w_in)


def sum_kernel(
    n, factor, dprojt, normed, cott, actt, w_in, out_in, out_out, out_normed,
    part_r, part_e, land_r, land_e, land_x, final_r, land_p, land_o, share, land_s, w_now,
    ring_r, ring_x, halves, pair_r, core_r, core_o, spread, core_s, fetch,
):
    grp = lax.axis_index("grp")
    dp = lax.axis_index("dp")
    x, core = grp // 2, lax.rem(grp, 2)
    half = n // 2
    up = lax.rem(dp, 2)
    pos = jnp.where(up == 0, dp // 2, n - 1 - dp // 2)

    def member(place):
        place = lax.rem(place + 2 * n, n)
        return jnp.where(place < half, 2 * place, 2 * (n - 1 - place) + 1)

    following, previous = (grp, member(pos + 1)), (grp, member(pos - 1))
    along_x = ((1 - x) * 2 + core, dp)
    other = (x * 2 + 1 - core, dp)
    greet([following, previous, along_x, other])
    onward = (following, previous)

    gi, go = dprojt.shape[1], cott.shape[1]
    rows_r = part_r.shape[1]
    rows_h, cols = land_e.shape[2:]
    split = rows_r - go
    spans = (slice(0, cols), slice(cols, 2 * cols))

    def dot(left, right, axes):
        return lax.dot_general(
            left, right, (((axes[0],), (axes[1],)), ((), ())),
            preferred_element_type=jnp.float32,
        )

    def owner(way, s):
        return member(pos - 1 - s) if way == 0 else member(pos + 1 + s)

    def compute_r(way, s):
        d = owner(way, s)
        part_r[way, :go] = dot(cott[d], actt[spans[way], :], (1, 1))
        part_r[way, go:] = dot(dprojt[d, :split], normed[:, spans[way]], (1, 0))

    def rows_of_half(h):
        return pl.ds(pl.multiple_of(split + h * rows_h, 16), rows_h)

    def compute_x(way, s, h):
        d = owner(way, s)
        return dot(dprojt[d, rows_of_half(h)], normed[:, spans[way]], (1, 0))

    def remote(src, dst, sems, where, device):
        return pltpu.make_async_remote_copy(
            src_ref=src, dst_ref=dst, send_sem=sems.at[(0,) + where],
            recv_sem=sems.at[(1,) + where], device_id=device, device_id_type=MESH,
        )

    streams = [(way, k) for k in range(2) for way in range(2)]
    cut_r, cut_x = rows_r // 16 * 8, rows_h // 16 * 8
    group_r = (slice(0, cut_r), slice(cut_r, rows_r))
    group_x = (slice(0, cut_x), slice(cut_x, rows_h))

    def hop_r(way, k, s, first=False):
        rows = group_r[k]
        src = final_r.at[way, rows] if first else land_r.at[way, s - 1, rows]
        return remote(src, land_r.at[way, s, rows], ring_r, (2 * way + k, s), onward[way])

    def hop_x(way, k, s, first=False):
        rows = group_x[k]
        src = land_e.at[0, way, rows] if first else land_x.at[way, s - 1, rows]
        return remote(src, land_x.at[way, s, rows], ring_x, (2 * way + k, s), onward[way])

    def give_half(s):
        return remote(part_e.at[s], land_e.at[s], halves, (s,), along_x)

    def loop(first, last, body):
        def step(s, carry):
            body(s)
            return carry

        lax.fori_loop(first, last, step, 0)

    for way in range(2):
        compute_r(way, 0)
        final_r[way] = part_r[way]
    for way, k in streams:
        hop_r(way, k, 0, True).start()

    def make_x(s):
        for way in range(2):
            part_e[s, way] = compute_x(way, s, 1 - x)
        give_half(s).start()

    loop(0, n, make_x)

    tokens = out_normed.shape[0]

    def add_share(d, k, total):
        copy = pltpu.make_async_copy(w_in.at[d, core], w_now, fetch)
        copy.start()
        copy.wait()
        rows = slice(k * tokens, (k + 1) * tokens)
        for span in spans:
            total[:, span] += dot(dprojt[d, :, rows], w_now[:, span], (0, 0))

    share[...] = jnp.zeros_like(share)
    loop(0, n, lambda d: add_share(d, 1, share))
    give_share = remote(share, land_s, core_s, (), other)
    give_share.start()

    def step_r(s):
        for way in range(2):
            compute_r(way, s + 1)
        for way, k in streams:
            hop_r(way, k, s, True).wait_recv()
            rows = group_r[k]
            land_r[way, s, rows] = land_r[way, s, rows] + part_r[way, rows]
            hop_r(way, k, s + 1).start()

    def step_first(s):
        step_r(s)
        add_share(s, 0, land_s)

    def own_x(way, s):
        return compute_x(way, s, x) + land_e[s, way]

    def step_x(s):
        give_half(s + 1).wait_recv()
        for way in range(2):
            land_e[s + 1, way] = own_x(way, s + 1)
        for way, k in streams:
            hop_x(way, k, s, True).wait_recv()
            rows = group_x[k]
            land_x[way, s, rows] = land_x[way, s, rows] + land_e[s + 1, way, rows]
            hop_x(way, k, s + 1).start()

    def step_both(s):
        step_r(s)
        step_x(s - lag)
        add_share(s, 0, land_s)

    lag = min(n // 2, n - 2)
    step_r(0)
    give_share.wait_recv()
    for d in (0, n - 2, n - 1):
        add_share(d, 0, land_s)
    loop(1, lag, step_first)
    give_half(0).wait_recv()
    for way in range(2):
        land_e[0, way] = own_x(way, 0)
    for way, k in streams:
        hop_x(way, k, 0, True).start()
    loop(lag, n - 2, step_both)

    out_normed[...] = land_s[...].astype(out_normed.dtype)

    def swap_r(way):
        return remote(part_r.at[way], land_p.at[way], pair_r, (way,), along_x)

    for way in range(2):
        compute_r(way, n - 1)
        for k in range(2):
            hop_r(way, k, n - 2, True).wait_recv()
        part_r[way] = (land_r[way, n - 2] + part_r[way]) * factor
        swap_r(way).start()

    loop(n - 2 - lag, n - 2, step_x)

    def tell_r(c, way):
        spot = out_in.at[c, :split, spans[way]]
        return remote(spot, spot, core_r, (way,), other)

    def tell_o(way):
        return remote(final_r.at[way, :go], land_o.at[way], core_o, (way,), other)

    def x_rows(h, k):
        start = split + h * rows_h + group_x[k].start
        return pl.ds(pl.multiple_of(start, 8), group_x[k].stop - group_x[k].start)

    def show(which, c, h, way, k, device):
        spot = out_in.at[c, x_rows(h, k), spans[way]]
        return remote(spot, spot, spread, (which, 2 * way + k), device)

    give_half(n - 1).wait_recv()
    for way in range(2):
        land_e[n - 1, way] = own_x(way, n - 1)
    for way, k in streams:
        hop_x(way, k, n - 2, True).wait_recv()
        rows = group_x[k]
        out_in[core, x_rows(x, k), spans[way]] = (
            land_x[way, n - 2, rows] + land_e[n - 1, way, rows]
        ) * factor
        show(0, core, x, way, k, along_x).start()
        show(1, core, x, way, k, other).start()
    for way in range(2):
        swap_r(way).wait_recv()
        for k in range(2):
            hop_r(way, k, 0, True).wait_send()
        final_r[way, :go] = part_r[way, :go] + land_p[way, :go]
        tell_o(way).start()
        out_in[core, :split, spans[way]] = part_r[way, go:] + land_p[way, go:]
        tell_r(core, way).start()
    for way, k in streams:
        show(0, core, 1 - x, way, k, along_x).wait_recv()
        show(2, core, 1 - x, way, k, other).start()
    for way in range(2):
        tell_o(way).wait_recv()
    mine = jnp.concatenate([final_r[0, :go], final_r[1, :go]], axis=1)
    theirs = jnp.concatenate([land_o[0], land_o[1]], axis=1)
    first = jnp.where(core == 0, mine, theirs)
    second = jnp.where(core == 0, theirs, mine)
    out_out[...] = jnp.concatenate(
        [
            block[:, b * gi : (b + 1) * gi]
            for b in range(half)
            for block in (first, second)
        ],
        axis=1,
    )
    for way in range(2):
        tell_r(1 - core, way).wait_recv()
    for way, k in streams:
        show(1, 1 - core, x, way, k, other).wait_recv()
        show(2, 1 - core, 1 - x, way, k, other).wait_recv()

    def drain(s):
        for way, k in streams:
            hop_r(way, k, s + 1).wait_send()
            hop_x(way, k, s, True).wait_send()

    loop(0, n - 2, drain)
    for way, k in streams:
        hop_x(way, k, n - 2, True).wait_send()
    loop(0, n, lambda s: give_half(s).wait_send())
    give_share.wait_send()
    for way in range(2):
        swap_r(way).wait_send()
        tell_o(way).wait_send()
        tell_r(core, way).wait_send()
    for way, k in streams:
        show(0, core, x, way, k, along_x).wait_send()
        show(1, core, x, way, k, other).wait_send()
        show(2, core, 1 - x, way, k, other).wait_send()


def sum_all(n, factor, dprojt, normed, cott, actt, w_in):
    gi, go, width = dprojt.shape[1], cott.shape[1], normed.shape[1]
    units = actt.shape[0]
    rows = gi + go
    rows_x = rows * 8 // 15 // 32 * 32
    rows_r, rows_h, cols = rows - rows_x, rows_x // 2, width // 2
    vmem = pl.BlockSpec(memory_space=pltpu.VMEM)
    f32 = jnp.float32
    dma = pltpu.SemaphoreType.DMA
    tokens = normed.shape[0] // 2
    return pl.pallas_call(
        functools.partial(sum_kernel, n, factor),
        out_shape=(
            jax.ShapeDtypeStruct((2, gi, width), f32),
            jax.ShapeDtypeStruct((go, 2 * units), f32),
            jax.ShapeDtypeStruct((tokens, width), jnp.bfloat16),
        ),
        in_specs=[vmem] * 4 + [pl.BlockSpec(memory_space=pl.ANY)],
        out_specs=(vmem,) * 3,
        scratch_shapes=[
            pltpu.VMEM((2, rows_r, cols), f32),
            pltpu.VMEM((n, 2, rows_h, cols), f32),
            pltpu.VMEM((2, n - 1, rows_r, cols), f32),
            pltpu.VMEM((n, 2, rows_h, cols), f32),
            pltpu.VMEM((2, n - 1, rows_h, cols), f32),
            pltpu.VMEM((2, rows_r, cols), f32),
            pltpu.VMEM((2, rows_r, cols), f32),
            pltpu.VMEM((2, go, cols), f32),
            pltpu.VMEM((tokens, width), f32),
            pltpu.VMEM((tokens, width), f32),
            pltpu.VMEM((gi, width), jnp.bfloat16),
            dma((2, 4, n - 1)),
            dma((2, 4, n - 1)),
            dma((2, n)),
            dma((2, 2)),
            dma((2, 2)),
            dma((2, 2)),
            dma((2, 3, 4)),
            dma((2,)),
            dma,
        ],
        compiler_params=pltpu.CompilerParams(
            collective_id=1, has_side_effects=True, vmem_limit_bytes=62 * 2**20
        ),
        cost_estimate=pl.CostEstimate(
            flops=6 * n * rows * tokens * width, bytes_accessed=20 * 2**20, transcendentals=0
        ),
        name="sum_gradients",
    )(dprojt, normed, cott, actt, w_in)


def local(normed, w_in, w_out, cotangent):
    width = w_out.shape[1]
    model = w_in.shape[1]
    n = lax.axis_size("dp")
    outer = lax.axis_size("grp")
    tokens = normed.shape[0]
    factor = (tokens * n * outer) ** (-0.5)
    gi = width // n
    blocks = w_in.reshape(n, 2, gi, model)
    both, cott, dprojt, actt = make_terms(n, normed, cotangent, w_out, blocks)
    grad_in, grad_out, grad_normed = sum_all(n, factor, dprojt, both, cott, actt, blocks)
    return (grad_in.reshape(2 * gi, model), grad_out, grad_normed)


def solution(mesh):
    placed = (P(("grp", "dp"), None), P(), P(), P(("grp", "dp"), None))
    return jax.shard_map(
        local,
        mesh=mesh,
        in_specs=placed,
        out_specs=(P("dp", None), P("dp", None), P(("grp", "dp"), None)),
        check_vma=False,
    )
```
